32 devices in a mesh: frame: 16 (over z, x, core), head: 2 (over y).
Axes of the slice: x: 2, y: 2, z: 4, core: 2. Of those that a mesh axis runs over, the one named last changes fastest.
Arguments:
- tokens: bfloat16 [2048, 5120], P('frame'), may hold values from -6 to 6
- w_query: bfloat16 [5120, 3072], P('frame', 'head')
- w_key: bfloat16 [5120, 3072], P('frame', 'head')
- w_value: bfloat16 [5120, 3072], P('frame', 'head'), may hold values from -0.078125 to 0.078125
- query_gain: float32 [3072], P('head')
- key_gain: float32 [3072], P('head')
- key_tiles: int32 [16, 8], replicated, may hold values from -1 to 15, as said below
Outputs:
- attended: bfloat16 [2048, 3072], P('frame', 'head')
The draws below stay inside these ranges and needn't reach their ends.
Inputs may be any that keep to these rules, and one draw needn't show every extreme that they name: Each frame index holds exactly one query tile, so tile t lives on frame index t. Row t of key_tiles names distinct key tiles first and is padded with -1 after them. A named tile u has u - t in 0, 1, -1, 2, -2 or plus or minus a power of two from 4 up to half the number of frame devices, and every tile with u - t in 0, 1, -1 that exists is named.
All inputs are finite; a program needn't handle non-finite values.
Results may differ from the reference program's by a relative error of at most 0.028.
Values may be sent and summed in bfloat16 or wider, within the bound.
A program may use at most 128 MiB of HBM per device.

```python
import math
import jax
import jax.numpy as jnp
from jax import lax

D = 5120
HEAD_DIM = 128
HEADS = 24
TILE = 128
TOK_DEV = 128
TOKENS = 2048
LIST = 8
N_FRAME = 16


def projection_pair(key):
    width = HEADS * HEAD_DIM
    head_of = jnp.arange(width) // HEAD_DIM
    ramp = 3.0 ** (head_of.astype(jnp.float32) / max(HEADS - 1, 1))
    rough_query = jnp.exp(jax.random.uniform(jax.random.fold_in(key, 7), (width,), jnp.float32, 0.0, math.log(10.0)))
    rough_key = jnp.exp(jax.random.uniform(jax.random.fold_in(key, 8), (width,), jnp.float32, 0.0, math.log(10.0)))
    base_query = jax.random.normal(jax.random.fold_in(key, 5), (D, width), jnp.float32) * D ** (-0.5)
    base_key = jax.random.normal(jax.random.fold_in(key, 6), (D, width), jnp.float32) * D ** (-0.5)
    base_query = base_query * (ramp * rough_query / 6.0)[None, :]
    base_key = base_key * (ramp * rough_key / 6.0)[None, :]
    return (base_query, base_key)


def draw_w_query(key, part):
    return projection_pair(key)[0].astype(jnp.bfloat16)


def draw_w_key(key, part):
    return projection_pair(key)[1].astype(jnp.bfloat16)


def gain_values(key):
    width = HEADS * HEAD_DIM
    return jnp.exp(jax.random.uniform(key, (width,), jnp.float32, math.log(0.5), math.log(2.0)))


def draw_query_gain(key, part):
    return gain_values(jax.random.fold_in(key, 31))


def draw_key_gain(key, part):
    return gain_values(jax.random.fold_in(key, 32))


def draw_key_tiles(key, part):
    tiles_per = TOK_DEV // TILE
    all_tiles = N_FRAME * tiles_per
    query_index = jnp.arange(all_tiles, dtype=jnp.int32)
    owner = query_index // tiles_per
    local_tiles = jnp.arange(tiles_per, dtype=jnp.int32)
    forced = query_index == N_FRAME // 2 * tiles_per
    tile_ids = []
    keep_flags = []
    for offset in (0, -1, 1):
        target = owner + offset
        inside = (target >= 0) & (target < N_FRAME)
        tile_ids.append(target[:, None] * tiles_per + local_tiles[None, :])
        keep_flags.append(jnp.broadcast_to(inside[:, None], (all_tiles, tiles_per)))
    for number, offset in enumerate((-2, 2)):
        target = owner + offset
        inside = (target >= 0) & (target < N_FRAME)
        coin_flip = jax.random.randint(jax.random.fold_in(key, 20 + number), (all_tiles, tiles_per), 0, 2)
        tile_ids.append(target[:, None] * tiles_per + local_tiles[None, :])
        keep_flags.append(inside[:, None] & ((coin_flip == 0) | forced[:, None]))
    stride = 4
    level_number = 2
    while stride <= N_FRAME // 2:
        for direction in (-1, 1):
            offset = direction * stride
            target = owner + offset
            inside = (target >= 0) & (target < N_FRAME)
            salt = 4 * level_number + (direction + 1) // 2
            chosen_tile = jax.random.randint(jax.random.fold_in(key, 100 + salt), (N_FRAME,), 0, tiles_per)
            coin_flip = jax.random.randint(jax.random.fold_in(key, 300 + salt), (all_tiles,), 0, stride // 2)
            tile_ids.append((target * tiles_per + chosen_tile[owner])[:, None])
            keep_flags.append((inside & ((coin_flip == 0) | forced))[:, None])
        stride = stride * 2
        level_number = level_number + 1
    tile_all = jnp.concatenate(tile_ids, axis=1).astype(jnp.int32)
    keep_all = jnp.concatenate(keep_flags, axis=1)
    entries = jnp.where(keep_all, tile_all, -1)
    positions = jnp.arange(tile_all.shape[1], dtype=jnp.int32)
    order_key = jnp.where(keep_all, 0, 1) * 100000 + positions[None, :]
    order = jnp.argsort(order_key, axis=1, stable=True)
    return jnp.take_along_axis(entries, order, axis=1)[:, :LIST].astype(jnp.int32)


def block_levels(stream_key, shape, cuts, low, high):
    def one(axis_at, parts):
        draws = jax.random.uniform(jax.random.fold_in(jax.random.fold_in(stream_key, 6), axis_at), (parts,), jnp.float32, low / len(cuts), high / len(cuts))
        return jnp.repeat(jnp.exp(draws), shape[axis_at] // parts).reshape((-1,) + (1,) * (len(shape) - axis_at - 1))

    level = one(*cuts[0])
    for cut in cuts[1:]:
        level = level * one(*cut)
    return level


def centred(stream_key, shape, spread, bound, pieces=(), kind=jnp.bfloat16):
    level = block_levels(stream_key, shape, pieces, -0.22, 0.18) if pieces else 1.0
    result = jax.random.normal(stream_key, shape, jnp.float32) * spread * level
    return jnp.minimum(jnp.maximum(result, -bound), bound).astype(kind)


def setup_inputs(seed: int = 0) -> dict:
    streams_of = jax.random.split(jax.random.key(seed), 8)
    tokens = centred(streams_of[0], (TOKENS, D), 1.0, 6.0, ((0, 16),))
    w_query = draw_w_query(jax.random.fold_in(streams_of[7], 71), 0)
    w_key = draw_w_key(jax.random.fold_in(streams_of[7], 71), 0)
    w_value = centred(streams_of[3], (D, HEADS * HEAD_DIM), D ** -0.5, 0.078125, ((0, 16), (1, 2)))
    query_gain = draw_query_gain(jax.random.fold_in(streams_of[7], 71), 0)
    key_gain = draw_key_gain(jax.random.fold_in(streams_of[7], 71), 0)
    key_tiles = draw_key_tiles(jax.random.fold_in(streams_of[7], 71), 0)
    return dict(tokens=tokens, w_query=w_query, w_key=w_key, w_value=w_value, query_gain=query_gain, key_gain=key_gain, key_tiles=key_tiles)


def normalize(values, gain):
    mean_square = lax.optimization_barrier(jnp.mean(values * values, axis=1))
    return (values * lax.rsqrt(mean_square + 1e-06)[:, None] * gain[None, :]).astype(jnp.bfloat16)

def reference(tokens, w_query, w_key, w_value, query_gain, key_gain, key_tiles):
    query = jnp.dot(tokens, w_query, preferred_element_type=jnp.float32)
    key_full = jnp.dot(tokens, w_key, preferred_element_type=jnp.float32)
    value_cast = jnp.dot(tokens, w_value, preferred_element_type=jnp.float32).astype(jnp.bfloat16)
    query_normed = normalize(query, query_gain)
    key_normed = normalize(key_full, key_gain)
    tile_count = tokens.shape[0] // TILE
    queries = query_normed.reshape(tile_count, TILE, HEADS, HEAD_DIM)
    keys_tiled = key_normed.reshape(tile_count, TILE, HEADS, HEAD_DIM)
    values_tiled = value_cast.reshape(tile_count, TILE, HEADS, HEAD_DIM)

    def one_tile(inputs):
        query_block, entries = inputs
        usable = entries >= 0
        clipped = jnp.where(usable, entries, 0).astype(jnp.int32)
        chosen_keys = keys_tiled[clipped].astype(jnp.float32)
        chosen_values = values_tiled[clipped].astype(jnp.float32)
        scores = jnp.einsum('qhd,ckhd->hqck', query_block.astype(jnp.float32), chosen_keys, precision=lax.Precision.HIGHEST) * HEAD_DIM ** (-0.5)
        scores = jnp.where(usable[None, None, :, None], scores, -jnp.inf)
        highest = lax.optimization_barrier(jnp.max(scores, axis=(2, 3), keepdims=True))
        raised = jnp.exp(scores - highest)
        softmax_weights = (raised / lax.optimization_barrier(jnp.sum(raised, axis=(2, 3), keepdims=True))).astype(jnp.bfloat16)
        combined = jnp.einsum('hqck,ckhd->qhd', softmax_weights.astype(jnp.float32), chosen_values, precision=lax.Precision.HIGHEST)
        return combined.astype(jnp.bfloat16)
    attended = lax.map(one_tile, (queries, key_tiles))
    return attended.reshape(tokens.shape[0], HEADS * HEAD_DIM)
```

```python
import functools

import jax
import jax.numpy as jnp
from jax import lax
from jax.experimental import pallas as pl
from jax.experimental.pallas import tpu as pltpu
from jax.sharding import PartitionSpec as P

HEAD_DIM = 128
HEADS = 24
TILE = 128
MESH = pl.DeviceIdType.MESH


def plan(frames, heads_here):
    groups = 4 if heads_here % 4 == 0 and frames % 8 == 0 else 1
    return groups, frames // groups


def candidates(frames):
    offsets = [0, 1, -1, 2, -2]
    stride = 4
    while stride < frames // 2:
        offsets += [stride, -stride]
        stride *= 2
    return tuple(offsets + [frames // 2] * (frames // 2 == stride))


def kernel(
    frames, groups, members, sides, offsets,
    tokens, w_query, w_key, w_value, query_gain, key_gain, key_tiles,
    out,
    tok, panel, full, query_normed, keys, values, stat_own, stat_in, sent, landed,
    local_sem, wz_send, wz_recv, tz_send, tz_recv, ty_send, ty_recv,
    wx_send, wx_recv, wc_send, wc_recv, st_send, st_recv,
    kx_send, kx_recv, kc_send, kc_recv, vx_send, vx_recv, vc_send, vc_recv,
    o_send, o_recv,
):
    index = lax.axis_index("frame")
    side = lax.axis_index("head")
    group, member = index // members, index % members
    chip, core = member // 2, member % 2
    chips = members // 2
    rows, width = tokens.shape
    depth = w_query.shape[0]
    part = w_query.shape[1] // groups
    group_depth = depth * members
    share = rows // sides

    def at(to_group, to_member, to_side):
        return (to_group * members + to_member, to_side)

    def other_group(step):
        return (group + step) % groups

    def back_group(step):
        return (group + groups - step) % groups

    def chip_member(step):
        return ((chip + step) % chips) * 2 + core

    def back_member(step):
        return ((chip + chips - step) % chips) * 2 + core

    mate = at(group, chip * 2 + 1 - core, side)

    peers = [mate]
    for step in range(1, chips):
        peers.append(at(group, chip_member(step), side))
    for step in range(groups):
        for turn in range(sides):
            if step or turn:
                peers.append(at(other_group(step), member, (side + turn) % sides))
    barrier = pltpu.get_barrier_semaphore()
    for peer in peers:
        pl.semaphore_signal(barrier, inc=1, device_id=peer, device_id_type=MESH)
    pl.semaphore_wait(barrier, len(peers))

    pending = []

    def send(src, dst, send_sem, recv_sem, device):
        copy = pltpu.make_async_remote_copy(
            src_ref=src, dst_ref=dst, send_sem=send_sem, recv_sem=recv_sem,
            device_id=device, device_id_type=MESH,
        )
        copy.start()
        pending.append(copy)
        return copy

    def member_rows(which):
        return pl.ds(pl.multiple_of(which * depth, depth), depth)

    weights = (w_query, w_key, w_value)

    def columns_of(which):
        return pl.ds(pl.multiple_of(which * part, part), part)

    local = []
    for i, weight in enumerate(weights):
        copy = pltpu.make_async_copy(
            weight.at[:, columns_of(group)],
            panel.at[group, member_rows(member), pl.ds(i * part, part)],
            local_sem.at[i],
        )
        copy.start()
        local.append(copy)
    wz = {}
    for step in range(1, groups):
        for i, weight in enumerate(weights):
            wz[step, i] = send(
                weight.at[:, columns_of(other_group(step))],
                panel.at[group, member_rows(member), pl.ds(i * part, part)],
                wz_send.at[step, i], wz_recv.at[step, i],
                at(other_group(step), member, side),
            )
    own = pltpu.make_async_copy(tokens, tok.at[group], local_sem.at[3])
    own.start()
    half = pl.ds(pl.multiple_of(side * share, share), share)
    tz = {}
    for step in range(1, groups):
        tz[step] = send(
            tokens.at[half], tok.at[group, half], tz_send.at[step], tz_recv.at[step],
            at(other_group(step), member, side),
        )

    for copy in local:
        copy.wait()
    wx, wc = {}, {}

    def spread(step):
        block = panel.at[back_group(step), member_rows(member)]
        for hop in range(1, chips):
            wx[step, hop] = send(
                block, block, wx_send.at[step, hop], wx_recv.at[step, hop],
                at(group, chip_member(hop), side),
            )
        wc[step, 0] = send(block, block, wc_send.at[step, 0], wc_recv.at[step, 0], mate)

    def relay(step):
        for hop in range(1, chips):
            wx[step, hop].wait_recv()
            block = panel.at[back_group(step), member_rows(back_member(hop))]
            wc[step, hop] = send(
                block, block, wc_send.at[step, hop], wc_recv.at[step, hop], mate
            )

    spread(0)
    for step in range(1, groups):
        for i in range(len(weights)):
            wz[step, i].wait_recv()
        spread(step)
        relay(step - 1)
    ty = {}
    for step in range(1, groups):
        tz[step].wait_recv()
        block = tok.at[back_group(step), half]
        for turn in range(1, sides):
            ty[step, turn] = send(
                block, block, ty_send.at[step, turn], ty_recv.at[step, turn],
                at(group, member, (side + turn) % sides),
            )
    relay(groups - 1)
    for step in range(groups):
        for hop in range(chips):
            wc[step, hop].wait_recv()
    own.wait()

    def project(which):
        @pl.loop(0, 3)
        def _(i):
            cols = pl.ds(pl.multiple_of(i * part, part), part)
            total = jnp.zeros((rows, part), jnp.float32)
            for g in range(groups):
                total += jnp.dot(
                    tok[which, :, g * group_depth:(g + 1) * group_depth],
                    panel[g, :, cols],
                    preferred_element_type=jnp.float32,
                )
            full[which, :, cols] = total

    project(group)
    for step in range(1, groups):
        for turn in range(1, sides):
            ty[step, turn].wait_recv()
        project(back_group(step))

    def gathered(buffer, x_send, x_recv, c_send, c_recv):
        block = buffer.at[member]
        across = [
            send(block, block, x_send.at[hop], x_recv.at[hop], at(group, chip_member(hop), side))
            for hop in range(1, chips)
        ]
        beside = [send(block, block, c_send.at[0], c_recv.at[0], mate)]

        def finish():
            for hop in range(1, chips):
                across[hop - 1].wait_recv()
                come = buffer.at[back_member(hop)]
                beside.append(send(come, come, c_send.at[hop], c_recv.at[hop], mate))
            return beside

        return finish

    first_row = lax.broadcasted_iota(jnp.int32, (8, TILE), 0) < 4
    for g in range(groups):
        spot = slice(g * rows, (g + 1) * rows)
        query = full[g, :, 0:part]
        key = full[g, :, part:2 * part]
        values[member, spot, :] = full[g, :, 2 * part:3 * part].astype(jnp.bfloat16)
        sums = []
        for value in (query, key):
            column = jnp.sum(value * value, axis=1, keepdims=True)
            sums.append(jnp.broadcast_to(column, (rows, TILE)).T[0:8, :])
        stat_own[:, spot] = jnp.where(first_row, sums[0], sums[1])
    st = []
    for step in range(groups):
        for turn in range(sides):
            if step or turn:
                slot = step * sides + turn
                st.append(send(
                    stat_own, stat_in.at[slot], st_send.at[slot], st_recv.at[slot],
                    at(other_group(step), member, (side + turn) % sides),
                ))
    finish_values = gathered(values, vx_send, vx_recv, vc_send, vc_recv)
    totals = stat_own[...]
    for slot in range(1, groups * sides):
        st[slot - 1].wait_recv()
        totals = totals + stat_in[slot]
    scales = lax.rsqrt(totals / (HEADS * HEAD_DIM) + 1e-06)
    q_gain = query_gain[pl.ds(group, 1), :]
    k_gain = key_gain[pl.ds(group, 1), :]

    def normed(value, row, gain):
        column = jnp.broadcast_to(row, (TILE, TILE)).T
        column = jnp.concatenate([column] * (part // TILE), axis=1)
        return (value * column * gain).astype(jnp.bfloat16)

    for g in range(groups):
        spot = slice(g * rows, (g + 1) * rows)
        keys[member, spot, :] = normed(full[g, :, part:2 * part], scales[4:5, spot], k_gain)
    finish_keys = gathered(keys, kx_send, kx_recv, kc_send, kc_recv)
    for g in range(groups):
        spot = slice(g * rows, (g + 1) * rows)
        query_normed[g] = normed(full[g, :, 0:part], scales[0:1, spot], q_gain)
    values_beside = finish_values()
    keys_beside = finish_keys()
    for copy in values_beside + keys_beside:
        copy.wait_recv()

    def attend(which, target):
        tile = which * members + member

        named = key_tiles[pl.ds(tile, 1), :]
        places, usable = [], []
        for offset in offsets:
            other = tile + offset
            place = (other + frames) % frames
            wanted = place if offset == frames // 2 else jnp.where(other < 0, -2, other)
            places.append((place // members, place % members))
            hits = jnp.where(named == wanted, 1.0, 0.0)
            usable.append(jnp.broadcast_to(jnp.max(hits, axis=1, keepdims=True), (TILE, TILE)))

        @pl.loop(0, part // HEAD_DIM)
        def _(head):
            cols = pl.ds(pl.multiple_of(head * HEAD_DIM, HEAD_DIM), HEAD_DIM)
            query = query_normed[which, :, cols]
            scores, parts = [], []
            for (other_part, other_member), use in zip(places, usable):
                spot = pl.ds(pl.multiple_of(other_part * TILE, TILE), TILE)
                key = keys[other_member, spot, cols]
                parts.append(values[other_member, spot, cols])
                score = lax.dot_general(
                    query, key, (((1,), (1,)), ((), ())), preferred_element_type=jnp.float32
                ) * HEAD_DIM ** (-0.5)
                scores.append(jnp.where(use > 0.5, score, -jnp.inf))
            scores = jnp.concatenate(scores, axis=1)
            highest = jnp.max(scores, axis=1, keepdims=True)
            raised = jnp.exp(scores - highest)
            softmax_weights = (raised / jnp.sum(raised, axis=1, keepdims=True)).astype(jnp.bfloat16)
            combined = jnp.dot(
                softmax_weights, jnp.concatenate(parts, axis=0), preferred_element_type=jnp.float32
            )
            target[:, cols] = combined.astype(jnp.bfloat16)

    outs = []
    for step in range(1, groups):
        attend(other_group(step), sent.at[step])
        outs.append(send(
            sent.at[step], landed.at[group], o_send.at[step], o_recv.at[step],
            at(other_group(step), member, side),
        ))
    attend(group, landed.at[group])
    for copy in outs:
        copy.wait_recv()
    for g in range(groups):
        out[:, g * part:(g + 1) * part] = landed[g]
    for copy in pending:
        copy.wait_send()


def on_device(tokens, w_query, w_key, w_value, query_gain, key_gain, key_tiles):
    frames, sides = lax.axis_size("frame"), lax.axis_size("head")
    rows, width = tokens.shape
    depth, columns = w_query.shape
    groups, members = plan(frames, columns // HEAD_DIM)
    chips = members // 2
    part = columns // groups
    dma = pltpu.SemaphoreType.DMA
    bf16, f32 = jnp.bfloat16, jnp.float32
    whole = pl.BlockSpec(memory_space=pltpu.VMEM)
    far = pl.BlockSpec(memory_space=pl.ANY)
    return pl.pallas_call(
        functools.partial(kernel, frames, groups, members, sides, candidates(frames)),
        out_shape=jax.ShapeDtypeStruct((rows, columns), bf16),
        in_specs=[far, far, far, far, whole, whole, whole],
        out_specs=whole,
        scratch_shapes=[
            pltpu.VMEM((groups, rows, width), bf16),
            pltpu.VMEM((groups, depth * members, 3 * part), bf16),
            pltpu.VMEM((groups, rows, 3 * part), f32),
            pltpu.VMEM((groups, rows, part), bf16),
            pltpu.VMEM((members, groups * rows, part), bf16),
            pltpu.VMEM((members, groups * rows, part), bf16),
            pltpu.VMEM((8, groups * rows), f32),
            pltpu.VMEM((groups * sides, 8, groups * rows), f32),
            pltpu.VMEM((groups, rows, part), bf16),
            pltpu.VMEM((groups, rows, part), bf16),
            dma((4,)),
            dma((groups, 3)), dma((groups, 3)),
            dma((groups,)), dma((groups,)),
            dma((groups, sides)), dma((groups, sides)),
            dma((groups, chips)), dma((groups, chips)),
            dma((groups, chips)), dma((groups, chips)),
            dma((groups * sides,)), dma((groups * sides,)),
            dma((chips,)), dma((chips,)), dma((chips,)), dma((chips,)),
            dma((chips,)), dma((chips,)), dma((chips,)), dma((chips,)),
            dma((groups,)), dma((groups,)),
        ],
        compiler_params=pltpu.CompilerParams(
            collective_id=0, has_side_effects=True, vmem_limit_bytes=48 * 1024 * 1024
        ),
        cost_estimate=pl.CostEstimate(
            flops=2 * rows * width * 3 * columns, bytes_accessed=20 * 1024 * 1024,
            transcendentals=0,
        ),
    )(
        tokens, w_query, w_key, w_value,
        query_gain.reshape(groups, part), key_gain.reshape(groups, part), key_tiles,
    )


def solution(mesh):
    return jax.shard_map(
        on_device,
        mesh=mesh,
        in_specs=(
            P("frame", None),
            P("frame", "head"),
            P("frame", "head"),
            P("frame", "head"),
            P("head"),
            P("head"),
            P(),
        ),
        out_specs=P("frame", "head"),
        check_vma=False,
    )
```

```python
import functools

import jax
import jax.numpy as jnp
from jax import lax
from jax.experimental import pallas as pl
from jax.experimental.pallas import tpu as pltpu
from jax.sharding import PartitionSpec as P

HEAD_DIM = 128
HEADS = 24
TILE = 128
MESH = pl.DeviceIdType.MESH


def plan(frames, heads_here):
    groups = 4 if heads_here % 4 == 0 and frames % 8 == 0 else 1
    return groups, frames // groups


def candidates(frames):
    offsets = [0, 1, -1, 2, -2]
    stride = 4
    while stride < frames // 2:
        offsets += [stride, -stride]
        stride *= 2
    return tuple(offsets + [frames // 2] * (frames // 2 == stride))


def kernel(
    frames, groups, members, sides, offsets,
    tokens, w_query, w_key, w_value, query_gain, key_gain, key_tiles,
    out,
    tok, panel, full, query_normed, keys, values, stat_own, stat_in, sent, landed,
    local_sem, wz_send, wz_recv, tz_send, tz_recv, ty_send, ty_recv,
    wx_send, wx_recv, wc_send, wc_recv, st_send, st_recv,
    kx_send, kx_recv, kc_send, kc_recv, vx_send, vx_recv, vc_send, vc_recv,
    o_send, o_recv,
):
    index = lax.axis_index("frame")
    side = lax.axis_index("head")
    group, member = index // members, index % members
    chip, core = member // 2, member % 2
    chips = members // 2
    rows, width = tokens.shape
    depth = w_query.shape[0]
    part = w_query.shape[1] // groups
    group_depth = depth * members
    share = rows // sides

    def at(to_group, to_member, to_side):
        return (to_group * members + to_member, to_side)

    def other_group(step):
        return (group + step) % groups

    def back_group(step):
        return (group + groups - step) % groups

    def chip_member(step):
        return ((chip + step) % chips) * 2 + core

    def back_member(step):
        return ((chip + chips - step) % chips) * 2 + core

    mate = at(group, chip * 2 + 1 - core, side)

    peers = [mate]
    for step in range(1, chips):
        peers.append(at(group, chip_member(step), side))
    for step in range(groups):
        for turn in range(sides):
            if step or turn:
                peers.append(at(other_group(step), member, (side + turn) % sides))
    barrier = pltpu.get_barrier_semaphore()
    for peer in peers:
        pl.semaphore_signal(barrier, inc=1, device_id=peer, device_id_type=MESH)
    pl.semaphore_wait(barrier, len(peers))

    pending = []

    def send(src, dst, send_sem, recv_sem, device):
        copy = pltpu.make_async_remote_copy(
            src_ref=src, dst_ref=dst, send_sem=send_sem, recv_sem=recv_sem,
            device_id=device, device_id_type=MESH,
        )
        copy.start()
        pending.append(copy)
        return copy

    def member_rows(which):
        return pl.ds(pl.multiple_of(which * depth, depth), depth)

    weights = (w_query, w_key, w_value)

    def columns_of(which):
        return pl.ds(pl.multiple_of(which * part, part), part)

    local = []
    for i, weight in enumerate(weights):
        copy = pltpu.make_async_copy(
            weight.at[:, columns_of(group)],
            panel.at[group, member_rows(member), pl.ds(i * part, part)],
            local_sem.at[i],
        )
        copy.start()
        local.append(copy)
    wz = {}
    for step in range(1, groups):
        for i, weight in enumerate(weights):
            wz[step, i] = send(
                weight.at[:, columns_of(other_group(step))],
                panel.at[group, member_rows(member), pl.ds(i * part, part)],
                wz_send.at[step, i], wz_recv.at[step, i],
                at(other_group(step), member, side),
            )
    own = pltpu.make_async_copy(tokens, tok.at[group], local_sem.at[3])
    own.start()
    half = pl.ds(pl.multiple_of(side * share, share), share)

    def has(which):
        return (which >= 0) & (which < groups)

    def tok_half(source):
        return tok.at[source, half]

    def hop_copy(way, k):
        source, to = group - way * k, group + way
        slot = (1 - way) // 2 * groups + k
        src = tokens.at[half] if k == 0 else tok_half(source)
        return has(source) & has(to), pltpu.make_async_remote_copy(
            src_ref=src, dst_ref=tok_half(source), send_sem=tz_send.at[slot],
            recv_sem=tz_recv.at[slot], device_id=at(to, member, side), device_id_type=MESH,
        )

    def swap_copies(way, k):
        slot = (1 - way) // 2 * groups + k
        block = tok_half(group - way * (k + 1))
        return [
            pltpu.make_async_remote_copy(
                src_ref=block, dst_ref=block, send_sem=ty_send.at[slot, turn],
                recv_sem=ty_recv.at[slot, turn],
                device_id=at(group, member, (side + turn) % sides), device_id_type=MESH,
            )
            for turn in range(1, sides)
        ]

    ways = [(way, k) for k in range(groups - 1) for way in (1, -1)]

    def start_hop(way, k):
        @pl.when(hop_copy(way, k)[0])
        def _():
            hop_copy(way, k)[1].start()

    for copy in local:
        copy.wait()
    wx, wc = {}, {}

    def spread(step):
        block = panel.at[back_group(step), member_rows(member)]
        for hop in range(1, chips):
            wx[step, hop] = send(
                block, block, wx_send.at[step, hop], wx_recv.at[step, hop],
                at(group, chip_member(hop), side),
            )
        wc[step, 0] = send(block, block, wc_send.at[step, 0], wc_recv.at[step, 0], mate)

    def relay(step):
        for hop in range(1, chips):
            wx[step, hop].wait_recv()
            block = panel.at[back_group(step), member_rows(back_member(hop))]
            wc[step, hop] = send(
                block, block, wc_send.at[step, hop], wc_recv.at[step, hop], mate
            )

    spread(0)
    for step in range(1, groups):
        for i in range(len(weights)):
            wz[step, i].wait_recv()
        spread(step)
        relay(step - 1)
    for copy in wz.values():
        copy.wait_send()
        pending.remove(copy)
    if groups > 1:
        start_hop(1, 0)
        start_hop(-1, 0)
    relay(groups - 1)
    for way, k in ways:
        @pl.when(has(group - way * (k + 1)))
        def _(way=way, k=k):
            hop_copy(way, k)[1].wait_recv()
            if k + 1 < groups - 1:
                start_hop(way, k + 1)
            for copy in swap_copies(way, k):
                copy.start()

    for step in range(groups):
        for hop in range(chips):
            wc[step, hop].wait_recv()
    own.wait()

    def project(which):
        @pl.loop(0, 3)
        def _(i):
            cols = pl.ds(pl.multiple_of(i * part, part), part)
            total = jnp.zeros((rows, part), jnp.float32)
            for g in range(groups):
                total += jnp.dot(
                    tok[which, :, g * group_depth:(g + 1) * group_depth],
                    panel[g, :, cols],
                    preferred_element_type=jnp.float32,
                )
            full[which, :, cols] = total

    project(group)
    for way, k in ways:
        @pl.when(has(group - way * (k + 1)))
        def _(way=way, k=k):
            for copy in swap_copies(way, k):
                copy.wait_recv()
            project(group - way * (k + 1))

    def gathered(buffer, x_send, x_recv, c_send, c_recv):
        block = buffer.at[member]
        across = [
            send(block, block, x_send.at[hop], x_recv.at[hop], at(group, chip_member(hop), side))
            for hop in range(1, chips)
        ]
        beside = [send(block, block, c_send.at[0], c_recv.at[0], mate)]

        def finish():
            for hop in range(1, chips):
                across[hop - 1].wait_recv()
                come = buffer.at[back_member(hop)]
                beside.append(send(come, come, c_send.at[hop], c_recv.at[hop], mate))
            return beside

        return finish

    first_row = lax.broadcasted_iota(jnp.int32, (8, TILE), 0) < 4
    for g in range(groups):
        spot = slice(g * rows, (g + 1) * rows)
        query = full[g, :, 0:part]
        key = full[g, :, part:2 * part]
        values[member, spot, :] = full[g, :, 2 * part:3 * part].astype(jnp.bfloat16)
        sums = []
        for value in (query, key):
            column = jnp.sum(value * value, axis=1, keepdims=True)
            sums.append(jnp.broadcast_to(column, (rows, TILE)).T[0:8, :])
        stat_own[:, spot] = jnp.where(first_row, sums[0], sums[1])
    st = []
    for step in range(groups):
        for turn in range(sides):
            if step or turn:
                slot = step * sides + turn
                st.append(send(
                    stat_own, stat_in.at[slot], st_send.at[slot], st_recv.at[slot],
                    at(other_group(step), member, (side + turn) % sides),
                ))
    finish_values = gathered(values, vx_send, vx_recv, vc_send, vc_recv)
    totals = stat_own[...]
    for slot in range(1, groups * sides):
        st[slot - 1].wait_recv()
        totals = totals + stat_in[slot]
    scales = lax.rsqrt(totals / (HEADS * HEAD_DIM) + 1e-06)
    q_gain = query_gain[pl.ds(group, 1), :]
    k_gain = key_gain[pl.ds(group, 1), :]

    def normed(value, row, gain):
        column = jnp.broadcast_to(row, (TILE, TILE)).T
        column = jnp.concatenate([column] * (part // TILE), axis=1)
        return (value * column * gain).astype(jnp.bfloat16)

    for g in range(groups):
        spot = slice(g * rows, (g + 1) * rows)
        keys[member, spot, :] = normed(full[g, :, part:2 * part], scales[4:5, spot], k_gain)
    finish_keys = gathered(keys, kx_send, kx_recv, kc_send, kc_recv)
    for g in range(groups):
        spot = slice(g * rows, (g + 1) * rows)
        query_normed[g] = normed(full[g, :, 0:part], scales[0:1, spot], q_gain)
    values_beside = finish_values()
    keys_beside = finish_keys()
    for copy in values_beside + keys_beside:
        copy.wait_recv()

    def attend(which, target):
        tile = which * members + member

        named = key_tiles[pl.ds(tile, 1), :]
        places, usable = [], []
        for offset in offsets:
            other = tile + offset
            place = (other + frames) % frames
            wanted = place if offset == frames // 2 else jnp.where(other < 0, -2, other)
            places.append((place // members, place % members))
            hits = jnp.where(named == wanted, 1.0, 0.0)
            usable.append(jnp.broadcast_to(jnp.max(hits, axis=1, keepdims=True), (TILE, TILE)))

        for head in range(part // HEAD_DIM):
            cols = pl.ds(head * HEAD_DIM, HEAD_DIM)
            query = query_normed[which, :, cols]
            scores, parts = [], []
            for (other_part, other_member), use in zip(places, usable):
                spot = pl.ds(pl.multiple_of(other_part * TILE, TILE), TILE)
                key = keys[other_member, spot, cols]
                parts.append(values[other_member, spot, cols])
                score = lax.dot_general(
                    query, key, (((1,), (1,)), ((), ())), preferred_element_type=jnp.float32
                ) * HEAD_DIM ** (-0.5)
                scores.append(jnp.where(use > 0.5, score, -jnp.inf))
            scores = jnp.concatenate(scores, axis=1)
            highest = jnp.max(scores, axis=1, keepdims=True)
            raised = jnp.exp(scores - highest)
            softmax_weights = (raised / jnp.sum(raised, axis=1, keepdims=True)).astype(jnp.bfloat16)
            combined = jnp.dot(
                softmax_weights, jnp.concatenate(parts, axis=0), preferred_element_type=jnp.float32
            )
            target[:, cols] = combined.astype(jnp.bfloat16)

    outs = []
    for step in range(1, groups):
        attend(other_group(step), sent.at[step])
        outs.append(send(
            sent.at[step], landed.at[group], o_send.at[step], o_recv.at[step],
            at(other_group(step), member, side),
        ))
    attend(group, landed.at[group])
    for copy in outs:
        copy.wait_recv()
    for g in range(groups):
        out[:, g * part:(g + 1) * part] = landed[g]
    for copy in pending:
        copy.wait_send()
    for way, k in ways:
        @pl.when(hop_copy(way, k)[0])
        def _(way=way, k=k):
            hop_copy(way, k)[1].wait_send()

        @pl.when(has(group - way * (k + 1)))
        def _(way=way, k=k):
            for copy in swap_copies(way, k):
                copy.wait_send()


def on_device(tokens, w_query, w_key, w_value, query_gain, key_gain, key_tiles):
    frames, sides = lax.axis_size("frame"), lax.axis_size("head")
    rows, width = tokens.shape
    depth, columns = w_query.shape
    groups, members = plan(frames, columns // HEAD_DIM)
    chips = members // 2
    part = columns // groups
    dma = pltpu.SemaphoreType.DMA
    bf16, f32 = jnp.bfloat16, jnp.float32
    whole = pl.BlockSpec(memory_space=pltpu.VMEM)
    far = pl.BlockSpec(memory_space=pl.ANY)
    return pl.pallas_call(
        functools.partial(kernel, frames, groups, members, sides, candidates(frames)),
        out_shape=jax.ShapeDtypeStruct((rows, columns), bf16),
        in_specs=[far, far, far, far, whole, whole, whole],
        out_specs=whole,
        scratch_shapes=[
            pltpu.VMEM((groups, rows, width), bf16),
            pltpu.VMEM((groups, depth * members, 3 * part), bf16),
            pltpu.VMEM((groups, rows, 3 * part), f32),
            pltpu.VMEM((groups, rows, part), bf16),
            pltpu.VMEM((members, groups * rows, part), bf16),
            pltpu.VMEM((members, groups * rows, part), bf16),
            pltpu.VMEM((8, groups * rows), f32),
            pltpu.VMEM((groups * sides, 8, groups * rows), f32),
            pltpu.VMEM((groups, rows, part), bf16),
            pltpu.VMEM((groups, rows, part), bf16),
            dma((4,)),
            dma((groups, 3)), dma((groups, 3)),
            dma((2 * groups,)), dma((2 * groups,)),
            dma((2 * groups, sides)), dma((2 * groups, sides)),
            dma((groups, chips)), dma((groups, chips)),
            dma((groups, chips)), dma((groups, chips)),
            dma((groups * sides,)), dma((groups * sides,)),
            dma((chips,)), dma((chips,)), dma((chips,)), dma((chips,)),
            dma((chips,)), dma((chips,)), dma((chips,)), dma((chips,)),
            dma((groups,)), dma((groups,)),
        ],
        compiler_params=pltpu.CompilerParams(
            collective_id=0, has_side_effects=True, vmem_limit_bytes=48 * 1024 * 1024
        ),
        cost_estimate=pl.CostEstimate(
            flops=2 * rows * width * 3 * columns, bytes_accessed=20 * 1024 * 1024,
            transcendentals=0,
        ),
    )(
        tokens, w_query, w_key, w_value,
        query_gain.reshape(groups, part), key_gain.reshape(groups, part), key_tiles,
    )


def solution(mesh):
    return jax.shard_map(
        on_device,
        mesh=mesh,
        in_specs=(
            P("frame", None),
            P("frame", "head"),
            P("frame", "head"),
            P("frame", "head"),
            P("head"),
            P("head"),
            P(),
        ),
        out_specs=P("frame", "head"),
        check_vma=False,
    )
```

```python
import functools

import jax
import jax.numpy as jnp
from jax import lax
from jax.experimental import pallas as pl
from jax.experimental.pallas import tpu as pltpu
from jax.sharding import PartitionSpec as P

HEAD_DIM = 128
HEADS = 24
TILE = 128
MESH = pl.DeviceIdType.MESH


def plan(frames, heads_here):
    groups = 4 if heads_here % 4 == 0 and frames % 8 == 0 else 1
    return groups, frames // groups


def candidates(frames):
    offsets = [0, 1, -1, 2, -2]
    stride = 4
    while stride < frames // 2:
        offsets += [stride, -stride]
        stride *= 2
    return tuple(offsets + [frames // 2] * (frames // 2 == stride))


def kernel(
    frames, groups, members, sides, offsets,
    tokens, w_query, w_key, w_value, query_gain, key_gain, key_tiles,
    out,
    tok, panel, full, query_normed, keys, values, stat_own, stat_in, sent, landed,
    local_sem, wz_send, wz_recv, tz_send, tz_recv, ty_send, ty_recv,
    wx_send, wx_recv, wc_send, wc_recv, st_send, st_recv,
    kx_send, kx_recv, kc_send, kc_recv, vx_send, vx_recv, vc_send, vc_recv,
    o_send, o_recv,
):
    index = lax.axis_index("frame")
    side = lax.axis_index("head")
    group, member = index // members, index % members
    chip, core = member // 2, member % 2
    chips = members // 2
    rows, width = tokens.shape
    depth = w_query.shape[0]
    part = w_query.shape[1] // groups
    group_depth = depth * members
    share = rows // sides

    def at(to_group, to_member, to_side):
        return (to_group * members + to_member, to_side)

    def other_group(step):
        return (group + step) % groups

    def back_group(step):
        return (group + groups - step) % groups

    def chip_member(step):
        return ((chip + step) % chips) * 2 + core

    def back_member(step):
        return ((chip + chips - step) % chips) * 2 + core

    mate = at(group, chip * 2 + 1 - core, side)

    peers = [mate]
    for step in range(1, chips):
        peers.append(at(group, chip_member(step), side))
    for step in range(groups):
        for turn in range(sides):
            if step or turn:
                peers.append(at(other_group(step), member, (side + turn) % sides))
    barrier = pltpu.get_barrier_semaphore()
    for peer in peers:
        pl.semaphore_signal(barrier, inc=1, device_id=peer, device_id_type=MESH)
    pl.semaphore_wait(barrier, len(peers))

    pending = []

    def send(src, dst, send_sem, recv_sem, device):
        copy = pltpu.make_async_remote_copy(
            src_ref=src, dst_ref=dst, send_sem=send_sem, recv_sem=recv_sem,
            device_id=device, device_id_type=MESH,
        )
        copy.start()
        pending.append(copy)
        return copy

    def member_rows(which):
        return pl.ds(pl.multiple_of(which * depth, depth), depth)

    weights = (w_query, w_key, w_value)

    def columns_of(which):
        return pl.ds(pl.multiple_of(which * part, part), part)

    local = []
    for i, weight in enumerate(weights):
        copy = pltpu.make_async_copy(
            weight.at[:, columns_of(group)],
            panel.at[group, member_rows(member), pl.ds(i * part, part)],
            local_sem.at[i],
        )
        copy.start()
        local.append(copy)
    wz = {}
    for step in range(1, groups):
        for i, weight in enumerate(weights):
            wz[step, i] = send(
                weight.at[:, columns_of(other_group(step))],
                panel.at[group, member_rows(member), pl.ds(i * part, part)],
                wz_send.at[step, i], wz_recv.at[step, i],
                at(other_group(step), member, side),
            )
    own = pltpu.make_async_copy(tokens, tok.at[group], local_sem.at[3])
    own.start()
    half = pl.ds(pl.multiple_of(side * share, share), share)

    def has(which):
        return (which >= 0) & (which < groups)

    def tok_half(source):
        return tok.at[source, half]

    def hop_copy(way, k):
        source, to = group - way * k, group + way
        slot = (1 - way) // 2 * groups + k
        src = tokens.at[half] if k == 0 else tok_half(source)
        return has(source) & has(to), pltpu.make_async_remote_copy(
            src_ref=src, dst_ref=tok_half(source), send_sem=tz_send.at[slot],
            recv_sem=tz_recv.at[slot], device_id=at(to, member, side), device_id_type=MESH,
        )

    def swap_copies(way, k):
        slot = (1 - way) // 2 * groups + k
        block = tok_half(group - way * (k + 1))
        return [
            pltpu.make_async_remote_copy(
                src_ref=block, dst_ref=block, send_sem=ty_send.at[slot, turn],
                recv_sem=ty_recv.at[slot, turn],
                device_id=at(group, member, (side + turn) % sides), device_id_type=MESH,
            )
            for turn in range(1, sides)
        ]

    ways = [(way, k) for k in range(groups - 1) for way in (1, -1)]

    def start_hop(way, k):
        @pl.when(hop_copy(way, k)[0])
        def _():
            hop_copy(way, k)[1].start()

    for copy in local:
        copy.wait()
    wx, wc = {}, {}

    def spread(step):
        block = panel.at[back_group(step), member_rows(member)]
        for hop in range(1, chips):
            wx[step, hop] = send(
                block, block, wx_send.at[step, hop], wx_recv.at[step, hop],
                at(group, chip_member(hop), side),
            )
        wc[step, 0] = send(block, block, wc_send.at[step, 0], wc_recv.at[step, 0], mate)

    def relay(step):
        for hop in range(1, chips):
            wx[step, hop].wait_recv()
            block = panel.at[back_group(step), member_rows(back_member(hop))]
            wc[step, hop] = send(
                block, block, wc_send.at[step, hop], wc_recv.at[step, hop], mate
            )

    spread(0)
    for step in range(1, groups):
        if step == groups - 1:
            start_hop(1, 0)
            start_hop(-1, 0)
        for i in range(len(weights)):
            wz[step, i].wait_recv()
        spread(step)
        relay(step - 1)
    relay(groups - 1)
    for way, k in ways:
        @pl.when(has(group - way * (k + 1)))
        def _(way=way, k=k):
            hop_copy(way, k)[1].wait_recv()
            if k + 1 < groups - 1:
                start_hop(way, k + 1)
            for copy in swap_copies(way, k):
                copy.start()

    for step in range(groups):
        for hop in range(chips):
            wc[step, hop].wait_recv()
    own.wait()

    def project(which):
        @pl.loop(0, 3)
        def _(i):
            cols = pl.ds(pl.multiple_of(i * part, part), part)
            total = jnp.zeros((rows, part), jnp.float32)
            for g in range(groups):
                total += jnp.dot(
                    tok[which, :, g * group_depth:(g + 1) * group_depth],
                    panel[g, :, cols],
                    preferred_element_type=jnp.float32,
                )
            full[which, :, cols] = total

    project(group)
    for way, k in ways:
        @pl.when(has(group - way * (k + 1)))
        def _(way=way, k=k):
            for copy in swap_copies(way, k):
                copy.wait_recv()
            project(group - way * (k + 1))

    def gathered(buffer, x_send, x_recv, c_send, c_recv):
        block = buffer.at[member]
        across = [
            send(block, block, x_send.at[hop], x_recv.at[hop], at(group, chip_member(hop), side))
            for hop in range(1, chips)
        ]
        beside = [send(block, block, c_send.at[0], c_recv.at[0], mate)]

        def finish():
            for hop in range(1, chips):
                across[hop - 1].wait_recv()
                come = buffer.at[back_member(hop)]
                beside.append(send(come, come, c_send.at[hop], c_recv.at[hop], mate))
            return beside

        return finish

    first_row = lax.broadcasted_iota(jnp.int32, (8, TILE), 0) < 4
    for g in range(groups):
        spot = slice(g * rows, (g + 1) * rows)
        query = full[g, :, 0:part]
        key = full[g, :, part:2 * part]
        values[member, spot, :] = full[g, :, 2 * part:3 * part].astype(jnp.bfloat16)
        sums = []
        for value in (query, key):
            column = jnp.sum(value * value, axis=1, keepdims=True)
            sums.append(jnp.broadcast_to(column, (rows, TILE)).T[0:8, :])
        stat_own[:, spot] = jnp.where(first_row, sums[0], sums[1])
    st = []
    for step in range(groups):
        for turn in range(sides):
            if step or turn:
                slot = step * sides + turn
                st.append(send(
                    stat_own, stat_in.at[slot], st_send.at[slot], st_recv.at[slot],
                    at(other_group(step), member, (side + turn) % sides),
                ))
    finish_values = gathered(values, vx_send, vx_recv, vc_send, vc_recv)
    totals = stat_own[...]
    for slot in range(1, groups * sides):
        st[slot - 1].wait_recv()
        totals = totals + stat_in[slot]
    scales = lax.rsqrt(totals / (HEADS * HEAD_DIM) + 1e-06)
    q_gain = query_gain[pl.ds(group, 1), :]
    k_gain = key_gain[pl.ds(group, 1), :]

    def normed(value, row, gain):
        column = jnp.broadcast_to(row, (TILE, TILE)).T
        column = jnp.concatenate([column] * (part // TILE), axis=1)
        return (value * column * gain).astype(jnp.bfloat16)

    for g in range(groups):
        spot = slice(g * rows, (g + 1) * rows)
        keys[member, spot, :] = normed(full[g, :, part:2 * part], scales[4:5, spot], k_gain)
    finish_keys = gathered(keys, kx_send, kx_recv, kc_send, kc_recv)
    for g in range(groups):
        spot = slice(g * rows, (g + 1) * rows)
        query_normed[g] = normed(full[g, :, 0:part], scales[0:1, spot], q_gain)
    values_beside = finish_values()
    keys_beside = finish_keys()
    for copy in values_beside + keys_beside:
        copy.wait_recv()

    def attend(which, target):
        tile = which * members + member

        named = key_tiles[pl.ds(tile, 1), :]
        places, usable = [], []
        for offset in offsets:
            other = tile + offset
            place = (other + frames) % frames
            wanted = place if offset == frames // 2 else jnp.where(other < 0, -2, other)
            places.append((place // members, place % members))
            hits = jnp.where(named == wanted, 1.0, 0.0)
            usable.append(jnp.broadcast_to(jnp.max(hits, axis=1, keepdims=True), (TILE, TILE)))

        for head in range(part // HEAD_DIM):
            cols = pl.ds(head * HEAD_DIM, HEAD_DIM)
            query = query_normed[which, :, cols]
            scores, parts = [], []
            for (other_part, other_member), use in zip(places, usable):
                spot = pl.ds(pl.multiple_of(other_part * TILE, TILE), TILE)
                key = keys[other_member, spot, cols]
                parts.append(values[other_member, spot, cols])
                score = lax.dot_general(
                    query, key, (((1,), (1,)), ((), ())), preferred_element_type=jnp.float32
                ) * HEAD_DIM ** (-0.5)
                scores.append(jnp.where(use > 0.5, score, -jnp.inf))
            scores = jnp.concatenate(scores, axis=1)
            highest = jnp.max(scores, axis=1, keepdims=True)
            raised = jnp.exp(scores - highest)
            softmax_weights = (raised / jnp.sum(raised, axis=1, keepdims=True)).astype(jnp.bfloat16)
            combined = jnp.dot(
                softmax_weights, jnp.concatenate(parts, axis=0), preferred_element_type=jnp.float32
            )
            target[:, cols] = combined.astype(jnp.bfloat16)

    outs = []
    for step in range(1, groups):
        attend(other_group(step), sent.at[step])
        outs.append(send(
            sent.at[step], landed.at[group], o_send.at[step], o_recv.at[step],
            at(other_group(step), member, side),
        ))
    attend(group, landed.at[group])
    for copy in outs:
        copy.wait_recv()
    for g in range(groups):
        out[:, g * part:(g + 1) * part] = landed[g]
    for copy in pending:
        copy.wait_send()
    for way, k in ways:
        @pl.when(hop_copy(way, k)[0])
        def _(way=way, k=k):
            hop_copy(way, k)[1].wait_send()

        @pl.when(has(group - way * (k + 1)))
        def _(way=way, k=k):
            for copy in swap_copies(way, k):
                copy.wait_send()


def on_device(tokens, w_query, w_key, w_value, query_gain, key_gain, key_tiles):
    frames, sides = lax.axis_size("frame"), lax.axis_size("head")
    rows, width = tokens.shape
    depth, columns = w_query.shape
    groups, members = plan(frames, columns // HEAD_DIM)
    chips = members // 2
    part = columns // groups
    dma = pltpu.SemaphoreType.DMA
    bf16, f32 = jnp.bfloat16, jnp.float32
    whole = pl.BlockSpec(memory_space=pltpu.VMEM)
    far = pl.BlockSpec(memory_space=pl.ANY)
    return pl.pallas_call(
        functools.partial(kernel, frames, groups, members, sides, candidates(frames)),
        out_shape=jax.ShapeDtypeStruct((rows, columns), bf16),
        in_specs=[far, far, far, far, whole, whole, whole],
        out_specs=whole,
        scratch_shapes=[
            pltpu.VMEM((groups, rows, width), bf16),
            pltpu.VMEM((groups, depth * members, 3 * part), bf16),
            pltpu.VMEM((groups, rows, 3 * part), f32),
            pltpu.VMEM((groups, rows, part), bf16),
            pltpu.VMEM((members, groups * rows, part), bf16),
            pltpu.VMEM((members, groups * rows, part), bf16),
            pltpu.VMEM((8, groups * rows), f32),
            pltpu.VMEM((groups * sides, 8, groups * rows), f32),
            pltpu.VMEM((groups, rows, part), bf16),
            pltpu.VMEM((groups, rows, part), bf16),
            dma((4,)),
            dma((groups, 3)), dma((groups, 3)),
            dma((2 * groups,)), dma((2 * groups,)),
            dma((2 * groups, sides)), dma((2 * groups, sides)),
            dma((groups, chips)), dma((groups, chips)),
            dma((groups, chips)), dma((groups, chips)),
            dma((groups * sides,)), dma((groups * sides,)),
            dma((chips,)), dma((chips,)), dma((chips,)), dma((chips,)),
            dma((chips,)), dma((chips,)), dma((chips,)), dma((chips,)),
            dma((groups,)), dma((groups,)),
        ],
        compiler_params=pltpu.CompilerParams(
            collective_id=0, has_side_effects=True, vmem_limit_bytes=48 * 1024 * 1024
        ),
        cost_estimate=pl.CostEstimate(
            flops=2 * rows * width * 3 * columns, bytes_accessed=20 * 1024 * 1024,
            transcendentals=0,
        ),
    )(
        tokens, w_query, w_key, w_value,
        query_gain.reshape(groups, part), key_gain.reshape(groups, part), key_tiles,
    )


def solution(mesh):
    return jax.shard_map(
        on_device,
        mesh=mesh,
        in_specs=(
            P("frame", None),
            P("frame", "head"),
            P("frame", "head"),
            P("frame", "head"),
            P("head"),
            P("head"),
            P(),
        ),
        out_specs=P("frame", "head"),
        check_vma=False,
    )
```
